32 devices in a mesh: groups: 2 (over y), expert: 16 (over z, x, core).
Axes of the slice: x: 2, y: 2, z: 4, core: 2. Of those that a mesh axis runs over, the one named last changes fastest.
Arguments:
- tokens: bfloat16 [4096, 3584], P(('groups', 'expert')), parts along dimension 0, may hold values from -6 to 6
- routes: int32 [4096, 2], P(('groups', 'expert')), parts along dimension 0, may hold values from 0 to 3, all different within a row; in each aligned block of 128 rows (0 to 127, 128 to 255, ...) at most 96 rows name the same one
- gates: float32 [4096, 2], P(('groups', 'expert')), parts along dimension 0, may hold values from 0.25 to 1
- gate_weight: bfloat16 [3584, 4096], P(None, 'expert'), may hold values from -0.09375 to 0.09375
- up_weight: bfloat16 [3584, 4096], P(None, 'expert'), may hold values from -0.09375 to 0.09375
- down_weight: bfloat16 [4096, 3584], P('expert'), may hold values from -0.1875 to 0.1875
Outputs:
- combined: bfloat16 [4096, 3584], P(('groups', 'expert')), parts along dimension 0
The draws below stay inside these ranges and needn't reach their ends.
There are 2 independent parts, one for each index of `groups`. The reference program is written for one: setup_inputs(seed, part) draws one part's arguments, and reference() takes and returns one part's arrays. A program takes and returns all parts, laid end to end along the dimension named above; an argument that names none is the same for every part. Nothing has to cross between parts.
Inputs may be any that keep to these rules, and one draw needn't show every extreme that they name: `routes`: each row names 2 different experts; in the rows of one device no expert is named more than 96 times, and in some block some expert exactly 96 times.
All inputs are finite; a program needn't handle non-finite values.
Results may differ from the reference program's by a relative error of at most 0.0071.
Values may be sent and summed in bfloat16 or wider, within the bound.
A program may use at most 128 MiB of HBM per device.

```python
import math
import jax
import jax.numpy as jnp
import numpy as np
from jax import lax

D = 3584
FF = 1024
HB = 128
SHARDS = 4
TOPK = 2
TOK_DEV = 128
EXP_LIVE = 4
H_DEV = 256
CAP = 96
TOKENS = 2048
N_EXPERT = 16


def levels(stream_key, shape, pieces, smallest, largest):
    def one(axis_at, shards_of):
        steps = jax.random.uniform(jax.random.fold_in(jax.random.fold_in(stream_key, 6), axis_at), (shards_of,), jnp.float32, smallest / len(pieces), largest / len(pieces))
        return jnp.repeat(jnp.exp(steps), shape[axis_at] // shards_of).reshape((-1,) + (1,) * (len(shape) - axis_at - 1))

    gain = one(*pieces[0])
    for cut in pieces[1:]:
        gain = gain * one(*cut)
    return gain


def deal_out(own_key, own, number, rows, number_of, top, reach, skew):
    ranking = jax.random.permutation(own_key, number_of)
    packed, usual = shares(number_of, rows * top, reach, skew, True), shares(number_of, rows * top, reach, skew, False)
    places = jnp.arange(number_of)

    def named(sizes, offset_by):
        used = int((sizes > 0).sum())
        fixed = max(1, used // 4)
        shifted = fixed + (places - fixed + offset_by * (used - fixed)) % max(1, number_of - fixed)
        return jnp.zeros((number_of,), jnp.int32).at[ranking[jnp.where(places < fixed, places, shifted)]].set(jnp.asarray(sizes, jnp.int32))

    sizes = jnp.where(number % 4 == 0, named(packed, number // 4), named(usual, number - number // 4 - 1))
    mixed = jax.random.permutation(jax.random.fold_in(own, 3), number_of)
    source_of, taker = mixed[0:number_of // 2 * 2:2], mixed[1:number_of // 2 * 2:2]
    slack = jnp.minimum(sizes[source_of] - 1, reach - sizes[taker]) // 2
    slack = jnp.where((source_of == ranking[0]) | (taker == ranking[0]) | (sizes[taker] == 0), 0, jnp.maximum(slack, 0))
    shifted = jax.random.randint(jax.random.fold_in(own, 4), (number_of // 2,), 0, 1 << 20) % (slack + 1)
    sizes = sizes.at[source_of].add(-shifted).at[taker].add(shifted)
    labels = jnp.searchsorted(jnp.cumsum(sizes), jnp.arange(rows * top), side="right").astype(jnp.int32)
    table = labels.reshape(top, rows).T
    table = table[jax.random.permutation(jax.random.fold_in(own, 1), rows)]
    offset_by = jax.random.randint(jax.random.fold_in(own, 2), (rows, 1), 0, top)
    return jnp.take_along_axis(table, (jnp.arange(top)[None, :] + offset_by) % top, axis=1)


def shares(count, total, most, lean, full):
    loads = [(1 << 20) // math.isqrt(grade ** lean) + 1 for grade in range(1, count + 1)]
    largest = most if full else min(most, max(-(-total // count), total * loads[0] // sum(loads)))
    least = 1 if total - largest >= count - 1 else 0
    counts, spare = [largest] + [least] * (count - 1), total - largest - least * (count - 1)
    while spare > 0:
        movable = [i for i in range(1, count) if counts[i] < largest] or [i for i in range(1, count) if counts[i] < most]
        whole, left = sum([loads[i] for i in movable]), spare
        for i in movable:
            addition = min(most - counts[i], max(1, left * loads[i] // whole), spare)
            counts[i] = counts[i] + addition
            spare = spare - addition
    return np.array(counts)


def scatter_about(stream_key, shape, deviation, bound, shards=(), kind=jnp.bfloat16):
    values = jax.random.normal(stream_key, shape, jnp.float32) * deviation
    if len(shards) > 0:
        values = levels(stream_key, shape, shards, -0.22, 0.18) * values
    return jnp.clip(values, min=-bound, max=bound).astype(kind)


def setup_inputs(seed: int = 0, part: int = 0) -> dict:
    seeds = jax.random.split(jax.random.key(seed), 7)
    part_keys = jax.random.split(jax.random.fold_in(seeds[6], part), 7)
    tokens = scatter_about(part_keys[0], (TOKENS, D), 1.0, 6.0, ((0, 16),))
    routes_keys = jax.random.split(jax.random.fold_in(part_keys[1], 1), TOKENS // TOK_DEV)
    routes_turns = jax.random.permutation(jax.random.fold_in(part_keys[1], 3), TOKENS // TOK_DEV)
    routes = jax.vmap(lambda own, number: deal_out(jax.random.fold_in(part_keys[1], 2), own, number, TOK_DEV, EXP_LIVE, TOPK, CAP, 2))(routes_keys, routes_turns).reshape((TOKENS, TOPK))
    gates = jnp.clip(0.25 + 0.75 * jax.random.uniform(part_keys[2], (TOKENS, TOPK), jnp.float32) ** levels(part_keys[2], (TOKENS, TOPK), ((0, 16),), -0.2, 0.2), 0.25, 1.0)
    gate_weight = scatter_about(seeds[3], (D, EXP_LIVE * FF), D ** -0.5, 0.09375, ((1, 16),))
    up_weight = scatter_about(seeds[4], (D, EXP_LIVE * FF), D ** -0.5, 0.09375, ((1, 16),))
    down_weight = scatter_about(seeds[5], (EXP_LIVE * FF, D), FF ** -0.5, 0.1875, ((0, 16),))
    return dict(tokens=tokens, routes=routes, gates=gates, gate_weight=gate_weight, up_weight=up_weight, down_weight=down_weight)


def hadamard(size):
    counter = jnp.arange(size, dtype=jnp.int32)
    parity = jnp.zeros((size, size), jnp.int32)
    for bit_level in range(size.bit_length() - 1):
        parity = parity + ((counter[:, None] >> bit_level) & (counter[None, :] >> bit_level) & 1)
    return (1 - 2 * (parity % 2)).astype(jnp.float32)


def rotate(tokens):
    row_count, width = tokens.shape
    blocked = tokens.reshape(row_count, width // HB, HB).astype(jnp.float32)
    turned = jnp.einsum("tbi,ij->tbj", blocked, hadamard(HB))
    return (turned * (1.0 / HB ** 0.5)).astype(jnp.bfloat16).reshape(row_count, width)


def reference(tokens, routes, gates, gate_weight, up_weight, down_weight):
    total, width = tokens.shape
    rotated = rotate(tokens)
    source = jnp.arange(total, dtype=jnp.int32) // TOK_DEV
    onehot = (routes.reshape(N_EXPERT, TOK_DEV * TOPK)[:, :, None] == jnp.arange(EXP_LIVE, dtype=jnp.int32)[None, None, :]).astype(jnp.int32)
    running = jnp.cumsum(onehot, axis=1) - onehot
    slot = jnp.sum(running * onehot, axis=-1).reshape(total, TOPK)
    target_slot = source[:, None] * CAP + slot
    filler = N_EXPERT * CAP

    def per_expert(accum, expert_id):
        chosen = routes == expert_id
        target = jnp.where(chosen, target_slot, filler).astype(jnp.int32)
        slot_rows = jnp.zeros((filler + 1, width), jnp.bfloat16).at[target].set(rotated[:, None, :])
        slot_rows = slot_rows[:filler]
        start = (expert_id * FF).astype(jnp.int32)
        gate_cols = lax.dynamic_slice_in_dim(gate_weight, start, FF, 1)
        up_cols = lax.dynamic_slice_in_dim(up_weight, start, FF, 1)
        down_rows = lax.dynamic_slice_in_dim(down_weight, start, FF, 0)
        gate_act = jnp.dot(slot_rows, gate_cols, preferred_element_type=jnp.float32)
        up_act = jnp.dot(slot_rows, up_cols, preferred_element_type=jnp.float32)
        hidden = (jax.nn.silu(gate_act) * up_act).astype(jnp.bfloat16)
        expert_sum = jnp.zeros((filler, width), jnp.float32)
        for shard_index in range(SHARDS):
            lower = shard_index * H_DEV
            partial_value = jnp.dot(hidden[:, lower:lower + H_DEV], down_rows[lower:lower + H_DEV], preferred_element_type=jnp.float32).astype(jnp.bfloat16)
            partial_value = lax.optimization_barrier(partial_value)
            expert_sum = expert_sum + partial_value.astype(jnp.float32)
        expert_sum = jnp.concatenate([expert_sum, jnp.zeros((1, width), jnp.float32)], 0)
        picked = expert_sum[target]
        accum = accum + jnp.sum(gates[:, :, None] * picked, axis=1)
        return accum, None

    start_sum = jnp.zeros((total, width), jnp.float32)
    result, unused = lax.scan(per_expert, start_sum, jnp.arange(EXP_LIVE, dtype=jnp.int32))
    return result.astype(jnp.bfloat16)
```

```python
import functools
import jax
import jax.numpy as jnp
from jax import lax
from jax.experimental import pallas as pl
from jax.experimental.pallas import tpu as pltpu
from jax.sharding import PartitionSpec as P

HB = 128
SHARDS = 4
AHEAD = 2
MESH = pl.DeviceIdType.MESH


def hadamard(size):
    counter = jnp.arange(size, dtype=jnp.int32)
    parity = jnp.zeros((size, size), jnp.int32)
    for bit_level in range(size.bit_length() - 1):
        parity = parity + (counter[:, None] >> bit_level & counter[None, :] >> bit_level & 1)
    return (1 - 2 * (parity % 2)).astype(jnp.bfloat16)


def layer_kernel(
    planes, steps, tok_ref, wt_ref, had_ref, gate_ref, up_ref, down_ref, out_ref,
    tok, wts, wcol, gu, dn, hid, acc, from_lo, from_hi, outbox,
    own_sem, x_s, x_r, y_s, y_r, co_s, co_r, cx_s, cx_r, cy_s, cy_r,
    tu_s, td_s, t_r, wu_s, wd_s, w_r, r_s, lo_r, hi_r,
):
    me = lax.axis_index("expert")
    y = lax.axis_index("groups")
    z, x, c = me // 4, (me // 2) % 2, me % 2
    top = planes - 1
    rows, width = tok_ref.shape
    units = gate_ref.shape[1]
    shard, xshard = 2 * x + c, 2 * (1 - x) + c
    xpeer, cpeer = {"expert": z * 4 + xshard}, {"expert": z * 4 + 2 * x + 1 - c}
    ypeer = {"groups": 1 - y}
    hi_peer, lo_peer = {"expert": me + 4}, {"expert": me - 4}
    wrows, wcols = width // 2 // steps, width // steps
    cols = lambda q: pl.ds(pl.multiple_of(q * wcols, wcols), wcols)

    barrier = pltpu.get_barrier_semaphore()
    for peer in (xpeer, cpeer, ypeer):
        pl.semaphore_signal(barrier, inc=1, device_id=peer, device_id_type=MESH)

    @pl.when(z > 0)
    def _():
        pl.semaphore_signal(barrier, inc=1, device_id=lo_peer, device_id_type=MESH)

    @pl.when(z < top)
    def _():
        pl.semaphore_signal(barrier, inc=1, device_id=hi_peer, device_id_type=MESH)

    pl.semaphore_wait(barrier, 3 + jnp.where(z > 0, 1, 0) + jnp.where(z < top, 1, 0))

    def remote(src, dst, send, recv, peer):
        return pltpu.make_async_remote_copy(
            src_ref=src, dst_ref=dst, send_sem=send, recv_sem=recv,
            device_id=peer, device_id_type=MESH)

    def piece(kind, part, half, k):
        if kind < 2:
            row = pl.multiple_of(half * (width // 2) + k * wrows, wrows)
            return gu.at[part, kind, pl.ds(row, wrows), :]
        row = pl.multiple_of(part * units + half * (units // 2), units // 2)
        return dn.at[pl.ds(row, units // 2), cols(k)]

    def own_piece(kind, half, k):
        if kind < 2:
            row = pl.multiple_of(half * (width // 2) + k * wrows, wrows)
            return (gate_ref, up_ref)[kind].at[pl.ds(row, wrows), :]
        row = pl.multiple_of(half * (units // 2), units // 2)
        return down_ref.at[pl.ds(row, units // 2), cols(k)]

    def x_copy(kind, k):
        return remote(own_piece(kind, y, k), piece(kind, shard, y, k),
                      x_s.at[kind, k], x_r.at[kind, k], xpeer)

    def y_copy(kind, k):
        got = piece(kind, xshard, y, k)
        return remote(got, got, y_s.at[kind, k], y_r.at[kind, k], ypeer)

    def cx_copy(kind, k):
        got = piece(kind, xshard, y, k)
        return remote(got, got, cx_s.at[kind, k], cx_r.at[kind, k], cpeer)

    def cy_copy(kind, k):
        got = piece(kind, xshard, 1 - y, k)
        return remote(got, got, cy_s.at[kind, k], cy_r.at[kind, k], cpeer)

    own_rows = pl.ds(pl.multiple_of(shard * units, units), units)

    def own_to(kind):
        return (gu.at[shard, 0], gu.at[shard, 1], dn.at[own_rows, :])[kind]

    weights = (gate_ref, up_ref, down_ref)

    def own_core(kind):
        return remote(weights[kind], own_to(kind), co_s.at[kind], co_r.at[kind], cpeer)

    def own_local(kind):
        return pltpu.make_async_copy(weights[kind], own_to(kind), own_sem.at[kind])

    def tok_copy(block, q, up):
        part = tok.at[block, :, cols(q)]
        return remote(part, part, (tu_s if up else td_s).at[block, q], t_r.at[block, q],
                      hi_peer if up else lo_peer)

    def w_copy(block, up):
        part = wts.at[block]
        return remote(part, part, (wu_s if up else wd_s).at[block], w_r.at[block],
                      hi_peer if up else lo_peer)

    def ret_copy(home, q, up):
        return remote(outbox.at[home, :, cols(q)], (from_lo if up else from_hi).at[home, :, cols(q)],
                      r_s.at[home, q], (lo_r if up else hi_r).at[home, q],
                      hi_peer if up else lo_peer)

    for k in range(AHEAD):
        for kind in (0, 1):
            x_copy(kind, k).start()
    wts[z] = wt_ref[...]

    @pl.when(z < top)
    def _():
        w_copy(z, True).start()

    @pl.when(z > 0)
    def _():
        w_copy(z, False).start()

    had = had_ref[...]

    @pl.loop(0, steps)
    def _(q):
        for b in range(wcols // HB):
            at = pl.ds(pl.multiple_of(q * wcols + b * HB, HB), HB)
            turned = jnp.dot(tok_ref[:, at], had, preferred_element_type=jnp.float32)
            tok[z, :, at] = (turned * (1.0 / HB**0.5)).astype(jnp.bfloat16)

        @pl.when(z < top)
        def _():
            tok_copy(z, q, True).start()

        @pl.when(z > 0)
        def _():
            tok_copy(z, q, False).start()

    for kind in range(3):
        own_local(kind).start()
        own_core(kind).start()

    def relay(r, q):
        lo, hi = z - r, z + r

        @pl.when(lo >= 0)
        def _():
            tok_copy(lo, q, True).wait_recv()

            @pl.when(q == 0)
            def _():
                w_copy(lo, True).wait_recv()

            @pl.when(z < top)
            def _():
                tok_copy(lo, q, True).start()

                @pl.when(q == 0)
                def _():
                    w_copy(lo, True).start()

        @pl.when(hi <= top)
        def _():
            tok_copy(hi, q, False).wait_recv()

            @pl.when(q == 0)
            def _():
                w_copy(hi, False).wait_recv()

            @pl.when(z > 0)
            def _():
                tok_copy(hi, q, False).start()

                @pl.when(q == 0)
                def _():
                    w_copy(hi, False).start()

    def pass_x(kind, k):
        x_copy(kind, k).wait_recv()
        y_copy(kind, k).start()
        cx_copy(kind, k).start()

    def pass_y(kind, k):
        y_copy(kind, k).wait_recv()
        cy_copy(kind, k).start()

    @pl.loop(0, steps)
    def _(k):
        for kind in (0, 1):
            pass_x(kind, k)

            @pl.when(k < steps - AHEAD)
            def _():
                x_copy(kind, k + AHEAD).start()

            @pl.when(k >= steps - AHEAD)
            def _():
                if kind == 0:
                    x_copy(2, 2 * (k - (steps - AHEAD))).start()
                else:
                    x_copy(2, 2 * (k - (steps - AHEAD)) + 1).start()

            @pl.when(k > 0)
            def _():
                pass_y(kind, k - 1)

            t = 2 * k + kind
            relay(t // steps + 1, t % steps)

    for kind in (0, 1):
        pass_y(kind, steps - 1)

    def wait_weights(kind):
        own_local(kind).wait()
        own_core(kind).wait_recv()

        @pl.loop(0, steps)
        def _(k):
            cx_copy(kind, k).wait_recv()
            cy_copy(kind, k).wait_recv()

    turn = jnp.where(z < planes // 2, 1, planes - 1)
    home_of = lambda p: lax.rem(z + turn * p, planes)

    def make_hidden(p):
        block = home_of(p)
        lane = lax.broadcasted_iota(jnp.int32, (8, rows), 0)
        row = jnp.sum(jnp.where(lane == z, wts[block], 0.0), axis=0, keepdims=True)
        wcol[p] = jnp.transpose(jnp.broadcast_to(row, (rows, rows)))

        @pl.loop(0, SHARDS)
        def _(s):
            g = jnp.dot(tok[block], gu[s, 0], preferred_element_type=jnp.float32)
            u = jnp.dot(tok[block], gu[s, 1], preferred_element_type=jnp.float32)
            h = (g / (1.0 + jnp.exp(-g))) * u
            hid[p, :, pl.ds(pl.multiple_of(s * units, units), units)] = h.astype(jnp.bfloat16)

    wait_weights(0)
    wait_weights(1)

    @pl.loop(0, steps)
    def _(k):
        pass_x(2, k)

        @pl.when(k + 2 * AHEAD < steps)
        def _():
            x_copy(2, k + 2 * AHEAD).start()

        @pl.when(k > 0)
        def _():
            pass_y(2, k - 1)

        relay(planes - 1, k)

        @pl.when(k % 2 == 0)
        def _():
            @pl.when(k < 2 * (planes - 1))
            def _():
                make_hidden(k // 2)

    pass_y(2, steps - 1)
    wait_weights(2)

    def expert_rows(p, q):
        val = jnp.dot(hid[p], dn[:, cols(q)], preferred_element_type=jnp.float32)
        w = wcol[p]
        for b in range(wcols // HB):
            acc[:, b * HB:(b + 1) * HB] = val[:, b * HB:(b + 1) * HB] * w

    def give_back(p):
        home = home_of(p)

        @pl.loop(0, steps)
        def _(q):
            expert_rows(p, q)

            @pl.when((home > z) & (z > 0))
            def _():
                ret_copy(home, q, True).wait_recv()
                acc[...] += from_lo[home, :, cols(q)].astype(jnp.float32)

            @pl.when((home < z) & (z < top))
            def _():
                ret_copy(home, q, False).wait_recv()
                acc[...] += from_hi[home, :, cols(q)].astype(jnp.float32)

            outbox[home, :, cols(q)] = acc[...].astype(jnp.bfloat16)

            @pl.when(home > z)
            def _():
                ret_copy(home, q, True).start()

            @pl.when(home < z)
            def _():
                ret_copy(home, q, False).start()

    @pl.loop(1, planes)
    def _(p):
        @pl.when(p == planes - 1)
        def _():
            make_hidden(p)

        give_back(p)

    @pl.loop(0, steps)
    def _(q):
        expert_rows(0, q)

        @pl.when(z > 0)
        def _():
            ret_copy(z, q, True).wait_recv()
            acc[...] += from_lo[z, :, cols(q)].astype(jnp.float32)

        @pl.when(z < top)
        def _():
            ret_copy(z, q, False).wait_recv()
            acc[...] += from_hi[z, :, cols(q)].astype(jnp.float32)

        out_ref[:, cols(q)] = acc[...].astype(jnp.bfloat16)

    for kind in range(3):
        own_core(kind).wait_send()

        @pl.loop(0, steps)
        def _(k):
            x_copy(kind, k).wait_send()
            y_copy(kind, k).wait_send()
            cx_copy(kind, k).wait_send()
            cy_copy(kind, k).wait_send()

    @pl.loop(0, planes)
    def _(block):
        for up in (True, False):
            @pl.when((z < top) & (block <= z) if up else (z > 0) & (block >= z))
            def _():
                w_copy(block, up).wait_send()

                @pl.loop(0, steps)
                def _(q):
                    tok_copy(block, q, up).wait_send()

        @pl.when(block != z)
        def _():
            @pl.loop(0, steps)
            def _(q):
                ret_copy(block, q, True).wait_send()


def on_slice(planes, tokens, routes, gates, gate_weight, up_weight, down_weight):
    rows, width = tokens.shape
    units = gate_weight.shape[1]
    steps = 7
    lanes = jnp.arange(8, dtype=jnp.int32)[:, None, None]
    wt = jnp.sum(jnp.where(routes[None] == lanes, gates[None], 0.0), axis=2)
    vmem = pl.BlockSpec(memory_space=pltpu.VMEM)
    anywhere = pl.BlockSpec(memory_space=pl.ANY)
    dma = pltpu.SemaphoreType.DMA
    bf16, f32 = jnp.bfloat16, jnp.float32
    return pl.pallas_call(
        functools.partial(layer_kernel, planes, steps),
        out_shape=jax.ShapeDtypeStruct((rows, width), bf16),
        in_specs=[vmem] * 3 + [anywhere] * 3,
        out_specs=vmem,
        scratch_shapes=[
            pltpu.VMEM((planes, rows, width), bf16),
            pltpu.VMEM((planes, 8, rows), f32),
            pltpu.VMEM((planes, rows, rows), f32),
            pltpu.VMEM((SHARDS, 2, width, units), bf16),
            pltpu.VMEM((SHARDS * units, width), bf16),
            pltpu.VMEM((planes, rows, SHARDS * units), bf16),
            pltpu.VMEM((rows, width // steps), f32),
            pltpu.VMEM((planes, rows, width), bf16),
            pltpu.VMEM((planes, rows, width), bf16),
            pltpu.VMEM((planes, rows, width), bf16),
            dma((3,)),
            dma((3, steps)), dma((3, steps)),
            dma((3, steps)), dma((3, steps)),
            dma((3,)), dma((3,)),
            dma((3, steps)), dma((3, steps)),
            dma((3, steps)), dma((3, steps)),
            dma((planes, steps)), dma((planes, steps)), dma((planes, steps)),
            dma((planes,)), dma((planes,)), dma((planes,)),
            dma((planes, steps)), dma((planes, steps)), dma((planes, steps)),
        ],
        compiler_params=pltpu.CompilerParams(
            collective_id=0, has_side_effects=True, vmem_limit_bytes=56 * 2**20
        ),
    )(tokens, wt, hadamard(HB), gate_weight, up_weight, down_weight)


def rotate(tokens):
    row_count, width = tokens.shape
    blocked = tokens.reshape(row_count, width // HB, HB)
    turned = jnp.einsum("tbi,ij->tbj", blocked, hadamard(HB), preferred_element_type=jnp.float32)
    return (turned * (1.0 / HB**0.5)).astype(jnp.bfloat16).reshape(row_count, width)


def on_device(tokens, routes, gates, gate_weight, up_weight, down_weight):
    devices = lax.axis_size("expert")
    resident = devices // SHARDS
    row_count, width = tokens.shape
    per_token = routes.shape[1]
    capacity = SHARDS * max(1, 3 * row_count * per_token // (2 * resident * SHARDS))
    rotated = rotate(tokens)
    flat_routes = routes.reshape(-1)
    onehot = (flat_routes[:, None] == jnp.arange(resident, dtype=jnp.int32)[None, :]).astype(
        jnp.int32
    )
    running = jnp.cumsum(onehot, axis=0) - onehot
    slot = jnp.sum(running * onehot, axis=1)
    target_slot = flat_routes * capacity + slot
    owners = jnp.arange(row_count * per_token, dtype=jnp.int32) // per_token
    owner_table = jnp.full((resident * capacity,), row_count, jnp.int32).at[target_slot].set(owners)
    padded = jnp.concatenate([rotated, jnp.zeros((1, width), jnp.bfloat16)], 0)
    buckets = padded[owner_table].reshape(resident, capacity, width)
    copies = jnp.broadcast_to(buckets[:, None], (resident, SHARDS, capacity, width)).reshape(
        devices, capacity, width
    )
    received = lax.all_to_all(copies, "expert", split_axis=0, concat_axis=0, tiled=True)
    slot_rows = received.reshape(-1, width)
    gate_act = jnp.dot(slot_rows, gate_weight, preferred_element_type=jnp.float32)
    up_act = jnp.dot(slot_rows, up_weight, preferred_element_type=jnp.float32)
    hidden = (jax.nn.silu(gate_act) * up_act).astype(jnp.bfloat16)
    partial_value = jnp.dot(hidden, down_weight, preferred_element_type=jnp.float32).astype(
        jnp.bfloat16
    )
    partial_value = partial_value.reshape(received.shape)
    returned = lax.all_to_all(partial_value, "expert", split_axis=0, concat_axis=0, tiled=True)
    expert_out = jnp.sum(
        returned.reshape(resident, SHARDS, capacity, width).astype(jnp.float32), axis=1
    )
    expert_out = expert_out.reshape(resident * capacity, width)
    picked = expert_out[target_slot].reshape(row_count, per_token, width)
    return jnp.sum(gates[:, :, None] * picked, axis=1).astype(jnp.bfloat16)


def solution(mesh):
    devices = mesh.shape["expert"]
    planes = devices // SHARDS
    body = on_device
    if devices == 16 and mesh.shape["groups"] == 2:
        body = functools.partial(on_slice, planes)
    in_specs = (
        P(("groups", "expert"), None),
        P(("groups", "expert"), None),
        P(("groups", "expert"), None),
        P(None, "expert"),
        P(None, "expert"),
        P("expert", None),
    )
    out_specs = P(("groups", "expert"), None)
    return jax.shard_map(
        body, mesh=mesh, in_specs=in_specs, out_specs=out_specs, check_vma=False
    )
```

```python
import functools
import jax
import jax.numpy as jnp
from jax import lax
from jax.experimental import pallas as pl
from jax.experimental.pallas import tpu as pltpu
from jax.sharding import PartitionSpec as P

HB = 128
SHARDS = 4
AHEAD = 3
MESH = pl.DeviceIdType.MESH


def hadamard(size):
    counter = jnp.arange(size, dtype=jnp.int32)
    parity = jnp.zeros((size, size), jnp.int32)
    for bit_level in range(size.bit_length() - 1):
        parity = parity + (counter[:, None] >> bit_level & counter[None, :] >> bit_level & 1)
    return (1 - 2 * (parity % 2)).astype(jnp.bfloat16)


def layer_kernel(
    planes, steps, tok_ref, wt_ref, had_ref, gate_ref, up_ref, down_ref, out_ref,
    tok, wts, wcol, gu, dn, hid, acc, from_lo, from_hi, outbox,
    own_sem, x_s, x_r, y_s, y_r, co_s, co_r, cx_s, cx_r, cy_s, cy_r,
    tu_s, td_s, t_r, wu_s, wd_s, w_r, r_s, lo_r, hi_r,
):
    me = lax.axis_index("expert")
    y = lax.axis_index("groups")
    z, x, c = me // 4, (me // 2) % 2, me % 2
    top = planes - 1
    rows, width = tok_ref.shape
    units = gate_ref.shape[1]
    shard, xshard = 2 * x + c, 2 * (1 - x) + c
    xpeer, cpeer = {"expert": z * 4 + xshard}, {"expert": z * 4 + 2 * x + 1 - c}
    ypeer = {"groups": 1 - y}
    hi_peer, lo_peer = {"expert": me + 4}, {"expert": me - 4}
    wrows, wcols = width // 2 // steps, width // steps
    cols = lambda q: pl.ds(pl.multiple_of(q * wcols, wcols), wcols)

    barrier = pltpu.get_barrier_semaphore()
    for peer in (xpeer, cpeer, ypeer):
        pl.semaphore_signal(barrier, inc=1, device_id=peer, device_id_type=MESH)

    @pl.when(z > 0)
    def _():
        pl.semaphore_signal(barrier, inc=1, device_id=lo_peer, device_id_type=MESH)

    @pl.when(z < top)
    def _():
        pl.semaphore_signal(barrier, inc=1, device_id=hi_peer, device_id_type=MESH)

    pl.semaphore_wait(barrier, 3 + jnp.where(z > 0, 1, 0) + jnp.where(z < top, 1, 0))

    def remote(src, dst, send, recv, peer):
        return pltpu.make_async_remote_copy(
            src_ref=src, dst_ref=dst, send_sem=send, recv_sem=recv,
            device_id=peer, device_id_type=MESH)

    def piece(kind, part, half, k):
        if kind < 2:
            row = pl.multiple_of(half * (width // 2) + k * wrows, wrows)
            return gu.at[part, kind, pl.ds(row, wrows), :]
        row = pl.multiple_of(part * units + half * (units // 2), units // 2)
        return dn.at[pl.ds(row, units // 2), cols(k)]

    def own_piece(kind, half, k):
        if kind < 2:
            row = pl.multiple_of(half * (width // 2) + k * wrows, wrows)
            return (gate_ref, up_ref)[kind].at[pl.ds(row, wrows), :]
        row = pl.multiple_of(half * (units // 2), units // 2)
        return down_ref.at[pl.ds(row, units // 2), cols(k)]

    def x_copy(kind, k):
        return remote(own_piece(kind, y, k), piece(kind, shard, y, k),
                      x_s.at[kind, k], x_r.at[kind, k], xpeer)

    def y_copy(kind, k):
        got = piece(kind, xshard, y, k)
        return remote(got, got, y_s.at[kind, k], y_r.at[kind, k], ypeer)

    def cx_copy(kind, k):
        got = piece(kind, xshard, y, k)
        return remote(got, got, cx_s.at[kind, k], cx_r.at[kind, k], cpeer)

    def cy_copy(kind, k):
        got = piece(kind, xshard, 1 - y, k)
        return remote(got, got, cy_s.at[kind, k], cy_r.at[kind, k], cpeer)

    own_rows = pl.ds(pl.multiple_of(shard * units, units), units)

    def own_to(kind):
        return (gu.at[shard, 0], gu.at[shard, 1], dn.at[own_rows, :])[kind]

    weights = (gate_ref, up_ref, down_ref)

    def own_core(kind):
        return remote(weights[kind], own_to(kind), co_s.at[kind], co_r.at[kind], cpeer)

    def own_local(kind):
        return pltpu.make_async_copy(weights[kind], own_to(kind), own_sem.at[kind])

    def tok_copy(block, q, up):
        part = tok.at[block, :, cols(q)]
        return remote(part, part, (tu_s if up else td_s).at[block, q], t_r.at[block, q],
                      hi_peer if up else lo_peer)

    def w_copy(block, up):
        part = wts.at[block]
        return remote(part, part, (wu_s if up else wd_s).at[block], w_r.at[block],
                      hi_peer if up else lo_peer)

    def ret_copy(home, q, up):
        return remote(outbox.at[home, :, cols(q)], (from_lo if up else from_hi).at[home, :, cols(q)],
                      r_s.at[home, q], (lo_r if up else hi_r).at[home, q],
                      hi_peer if up else lo_peer)

    for k in range(AHEAD):
        for kind in (0, 1):
            x_copy(kind, k).start()
    wts[z] = wt_ref[...]

    @pl.when(z < top)
    def _():
        w_copy(z, True).start()

    @pl.when(z > 0)
    def _():
        w_copy(z, False).start()

    had = had_ref[...]

    @pl.loop(0, steps)
    def _(q):
        for b in range(wcols // HB):
            at = pl.ds(pl.multiple_of(q * wcols + b * HB, HB), HB)
            turned = jnp.dot(tok_ref[:, at], had, preferred_element_type=jnp.float32)
            tok[z, :, at] = (turned * (1.0 / HB**0.5)).astype(jnp.bfloat16)

        @pl.when(z < top)
        def _():
            tok_copy(z, q, True).start()

        @pl.when(z > 0)
        def _():
            tok_copy(z, q, False).start()

    for kind in range(3):
        own_local(kind).start()
        own_core(kind).start()

    def relay(r, q):
        lo, hi = z - r, z + r

        @pl.when(lo >= 0)
        def _():
            tok_copy(lo, q, True).wait_recv()

            @pl.when(q == 0)
            def _():
                w_copy(lo, True).wait_recv()

            @pl.when(z < top)
            def _():
                tok_copy(lo, q, True).start()

                @pl.when(q == 0)
                def _():
                    w_copy(lo, True).start()

        @pl.when(hi <= top)
        def _():
            tok_copy(hi, q, False).wait_recv()

            @pl.when(q == 0)
            def _():
                w_copy(hi, False).wait_recv()

            @pl.when(z > 0)
            def _():
                tok_copy(hi, q, False).start()

                @pl.when(q == 0)
                def _():
                    w_copy(hi, False).start()

    def pass_x(kind, k):
        x_copy(kind, k).wait_recv()
        y_copy(kind, k).start()
        cx_copy(kind, k).start()

    def pass_y(kind, k):
        y_copy(kind, k).wait_recv()
        cy_copy(kind, k).start()

    @pl.loop(0, steps)
    def _(k):
        for kind in (0, 1):
            pass_x(kind, k)

            @pl.when(k < steps - AHEAD)
            def _():
                x_copy(kind, k + AHEAD).start()

            @pl.when(k >= steps - AHEAD)
            def _():
                if kind == 0:
                    x_copy(2, 2 * (k - (steps - AHEAD))).start()
                else:
                    x_copy(2, 2 * (k - (steps - AHEAD)) + 1).start()

            @pl.when(k > 0)
            def _():
                pass_y(kind, k - 1)

            t = 2 * k + kind
            relay(t // steps + 1, t % steps)

    for kind in (0, 1):
        pass_y(kind, steps - 1)

    def wait_weights(kind):
        own_local(kind).wait()
        own_core(kind).wait_recv()

        @pl.loop(0, steps)
        def _(k):
            cx_copy(kind, k).wait_recv()
            cy_copy(kind, k).wait_recv()

    low = z < planes // 2

    def home_of(p):
        across = jnp.where(p == 1, jnp.where(low, 2, 1), jnp.where(low, 3, 0))
        beside = jnp.where(low, 1 - z, 5 - z)
        return jnp.where(p == 0, z, jnp.where(p == 3, beside, across))

    def make_hidden(p):
        block = home_of(p)
        lane = lax.broadcasted_iota(jnp.int32, (8, rows), 0)
        row = jnp.sum(jnp.where(lane == z, wts[block], 0.0), axis=0, keepdims=True)
        wcol[p] = jnp.transpose(jnp.broadcast_to(row, (rows, rows)))

        @pl.loop(0, SHARDS)
        def _(s):
            g = jnp.dot(tok[block], gu[s, 0], preferred_element_type=jnp.float32)
            u = jnp.dot(tok[block], gu[s, 1], preferred_element_type=jnp.float32)
            h = (g / (1.0 + jnp.exp(-g))) * u
            hid[p, :, pl.ds(pl.multiple_of(s * units, units), units)] = h.astype(jnp.bfloat16)

    def expert_rows(p, q):
        val = jnp.dot(hid[p], dn[:, cols(q)], preferred_element_type=jnp.float32)
        w = wcol[p]
        for b in range(wcols // HB):
            acc[:, b * HB:(b + 1) * HB] = val[:, b * HB:(b + 1) * HB] * w

    def give_back(p, q):
        home = home_of(p)
        expert_rows(p, q)

        @pl.when((home > z) & (z > 0))
        def _():
            ret_copy(home, q, True).wait_recv()
            acc[...] += from_lo[home, :, cols(q)].astype(jnp.float32)

        @pl.when((home < z) & (z < top))
        def _():
            ret_copy(home, q, False).wait_recv()
            acc[...] += from_hi[home, :, cols(q)].astype(jnp.float32)

        outbox[home, :, cols(q)] = acc[...].astype(jnp.bfloat16)

        @pl.when(home > z)
        def _():
            ret_copy(home, q, True).start()

        @pl.when(home < z)
        def _():
            ret_copy(home, q, False).start()

    wait_weights(0)
    wait_weights(1)
    own_local(2).wait()
    own_core(2).wait_recv()
    make_hidden(1)

    def first_back(q):
        cx_copy(2, q).wait_recv()
        cy_copy(2, q).wait_recv()
        give_back(1, q)

    @pl.loop(0, steps)
    def _(k):
        pass_x(2, k)

        @pl.when(k + 2 * AHEAD < steps)
        def _():
            x_copy(2, k + 2 * AHEAD).start()

        @pl.when(k > 0)
        def _():
            pass_y(2, k - 1)

        relay(planes - 1, k)

        @pl.when(k > 1)
        def _():
            first_back(k - 2)

    pass_y(2, steps - 1)
    first_back(steps - 2)
    first_back(steps - 1)

    @pl.loop(2, planes)
    def _(p):
        make_hidden(p)

        @pl.loop(0, steps)
        def _(q):
            give_back(p, q)

    make_hidden(0)

    @pl.loop(0, steps)
    def _(q):
        expert_rows(0, q)

        @pl.when(z > 0)
        def _():
            ret_copy(z, q, True).wait_recv()
            acc[...] += from_lo[z, :, cols(q)].astype(jnp.float32)

        @pl.when(z < top)
        def _():
            ret_copy(z, q, False).wait_recv()
            acc[...] += from_hi[z, :, cols(q)].astype(jnp.float32)

        out_ref[:, cols(q)] = acc[...].astype(jnp.bfloat16)

    for kind in range(3):
        own_core(kind).wait_send()

        @pl.loop(0, steps)
        def _(k):
            x_copy(kind, k).wait_send()
            y_copy(kind, k).wait_send()
            cx_copy(kind, k).wait_send()
            cy_copy(kind, k).wait_send()

    @pl.loop(0, planes)
    def _(block):
        for up in (True, False):
            @pl.when((z < top) & (block <= z) if up else (z > 0) & (block >= z))
            def _():
                w_copy(block, up).wait_send()

                @pl.loop(0, steps)
                def _(q):
                    tok_copy(block, q, up).wait_send()

        @pl.when(block != z)
        def _():
            @pl.loop(0, steps)
            def _(q):
                ret_copy(block, q, True).wait_send()


def on_slice(planes, tokens, routes, gates, gate_weight, up_weight, down_weight):
    rows, width = tokens.shape
    units = gate_weight.shape[1]
    steps = 7
    lanes = jnp.arange(8, dtype=jnp.int32)[:, None, None]
    wt = jnp.sum(jnp.where(routes[None] == lanes, gates[None], 0.0), axis=2)
    vmem = pl.BlockSpec(memory_space=pltpu.VMEM)
    anywhere = pl.BlockSpec(memory_space=pl.ANY)
    dma = pltpu.SemaphoreType.DMA
    bf16, f32 = jnp.bfloat16, jnp.float32
    return pl.pallas_call(
        functools.partial(layer_kernel, planes, steps),
        out_shape=jax.ShapeDtypeStruct((rows, width), bf16),
        in_specs=[vmem] * 3 + [anywhere] * 3,
        out_specs=vmem,
        scratch_shapes=[
            pltpu.VMEM((planes, rows, width), bf16),
            pltpu.VMEM((planes, 8, rows), f32),
            pltpu.VMEM((planes, rows, rows), f32),
            pltpu.VMEM((SHARDS, 2, width, units), bf16),
            pltpu.VMEM((SHARDS * units, width), bf16),
            pltpu.VMEM((planes, rows, SHARDS * units), bf16),
            pltpu.VMEM((rows, width // steps), f32),
            pltpu.VMEM((planes, rows, width), bf16),
            pltpu.VMEM((planes, rows, width), bf16),
            pltpu.VMEM((planes, rows, width), bf16),
            dma((3,)),
            dma((3, steps)), dma((3, steps)),
            dma((3, steps)), dma((3, steps)),
            dma((3,)), dma((3,)),
            dma((3, steps)), dma((3, steps)),
            dma((3, steps)), dma((3, steps)),
            dma((planes, steps)), dma((planes, steps)), dma((planes, steps)),
            dma((planes,)), dma((planes,)), dma((planes,)),
            dma((planes, steps)), dma((planes, steps)), dma((planes, steps)),
        ],
        compiler_params=pltpu.CompilerParams(
            collective_id=0, has_side_effects=True, vmem_limit_bytes=56 * 2**20
        ),
    )(tokens, wt, hadamard(HB), gate_weight, up_weight, down_weight)


def rotate(tokens):
    row_count, width = tokens.shape
    blocked = tokens.reshape(row_count, width // HB, HB)
    turned = jnp.einsum("tbi,ij->tbj", blocked, hadamard(HB), preferred_element_type=jnp.float32)
    return (turned * (1.0 / HB**0.5)).astype(jnp.bfloat16).reshape(row_count, width)


def on_device(tokens, routes, gates, gate_weight, up_weight, down_weight):
    devices = lax.axis_size("expert")
    resident = devices // SHARDS
    row_count, width = tokens.shape
    per_token = routes.shape[1]
    capacity = SHARDS * max(1, 3 * row_count * per_token // (2 * resident * SHARDS))
    rotated = rotate(tokens)
    flat_routes = routes.reshape(-1)
    onehot = (flat_routes[:, None] == jnp.arange(resident, dtype=jnp.int32)[None, :]).astype(
        jnp.int32
    )
    running = jnp.cumsum(onehot, axis=0) - onehot
    slot = jnp.sum(running * onehot, axis=1)
    target_slot = flat_routes * capacity + slot
    owners = jnp.arange(row_count * per_token, dtype=jnp.int32) // per_token
    owner_table = jnp.full((resident * capacity,), row_count, jnp.int32).at[target_slot].set(owners)
    padded = jnp.concatenate([rotated, jnp.zeros((1, width), jnp.bfloat16)], 0)
    buckets = padded[owner_table].reshape(resident, capacity, width)
    copies = jnp.broadcast_to(buckets[:, None], (resident, SHARDS, capacity, width)).reshape(
        devices, capacity, width
    )
    received = lax.all_to_all(copies, "expert", split_axis=0, concat_axis=0, tiled=True)
    slot_rows = received.reshape(-1, width)
    gate_act = jnp.dot(slot_rows, gate_weight, preferred_element_type=jnp.float32)
    up_act = jnp.dot(slot_rows, up_weight, preferred_element_type=jnp.float32)
    hidden = (jax.nn.silu(gate_act) * up_act).astype(jnp.bfloat16)
    partial_value = jnp.dot(hidden, down_weight, preferred_element_type=jnp.float32).astype(
        jnp.bfloat16
    )
    partial_value = partial_value.reshape(received.shape)
    returned = lax.all_to_all(partial_value, "expert", split_axis=0, concat_axis=0, tiled=True)
    expert_out = jnp.sum(
        returned.reshape(resident, SHARDS, capacity, width).astype(jnp.float32), axis=1
    )
    expert_out = expert_out.reshape(resident * capacity, width)
    picked = expert_out[target_slot].reshape(row_count, per_token, width)
    return jnp.sum(gates[:, :, None] * picked, axis=1).astype(jnp.bfloat16)


def solution(mesh):
    devices = mesh.shape["expert"]
    planes = devices // SHARDS
    body = on_device
    if devices == 16 and mesh.shape["groups"] == 2:
        body = functools.partial(on_slice, planes)
    in_specs = (
        P(("groups", "expert"), None),
        P(("groups", "expert"), None),
        P(("groups", "expert"), None),
        P(None, "expert"),
        P(None, "expert"),
        P("expert", None),
    )
    out_specs = P(("groups", "expert"), None)
    return jax.shard_map(
        body, mesh=mesh, in_specs=in_specs, out_specs=out_specs, check_vma=False
    )
```

```python
import functools
import jax
import jax.numpy as jnp
from jax import lax
from jax.experimental import pallas as pl
from jax.experimental.pallas import tpu as pltpu
from jax.sharding import PartitionSpec as P

HB = 128
SHARDS = 4
AHEAD = 3
MESH = pl.DeviceIdType.MESH


def hadamard(size):
    counter = jnp.arange(size, dtype=jnp.int32)
    parity = jnp.zeros((size, size), jnp.int32)
    for bit_level in range(size.bit_length() - 1):
        parity = parity + (counter[:, None] >> bit_level & counter[None, :] >> bit_level & 1)
    return (1 - 2 * (parity % 2)).astype(jnp.bfloat16)


def layer_kernel(
    planes, steps, cap, tok_ref, wt_ref, had_ref, gate_ref, up_ref, down_ref, out_ref,
    tok, wts, wcol, place, gu, dn, hid, acc, from_lo, from_hi, outbox,
    own_sem, x_s, x_r, y_s, y_r, co_s, co_r, cx_s, cx_r, cy_s, cy_r,
    tu_s, td_s, t_r, wu_s, wd_s, w_r, r_s, lo_r, hi_r,
):
    me = lax.axis_index("expert")
    y = lax.axis_index("groups")
    z, x, c = me // 4, (me // 2) % 2, me % 2
    top = planes - 1
    rows, width = tok_ref.shape
    units = gate_ref.shape[1]
    shard, xshard = 2 * x + c, 2 * (1 - x) + c
    xpeer, cpeer = {"expert": z * 4 + xshard}, {"expert": z * 4 + 2 * x + 1 - c}
    ypeer = {"groups": 1 - y}
    hi_peer, lo_peer = {"expert": me + 4}, {"expert": me - 4}
    wrows, wcols = width // 2 // steps, width // steps
    cols = lambda q: pl.ds(pl.multiple_of(q * wcols, wcols), wcols)

    barrier = pltpu.get_barrier_semaphore()
    for peer in (xpeer, cpeer, ypeer):
        pl.semaphore_signal(barrier, inc=1, device_id=peer, device_id_type=MESH)

    @pl.when(z > 0)
    def _():
        pl.semaphore_signal(barrier, inc=1, device_id=lo_peer, device_id_type=MESH)

    @pl.when(z < top)
    def _():
        pl.semaphore_signal(barrier, inc=1, device_id=hi_peer, device_id_type=MESH)

    pl.semaphore_wait(barrier, 3 + jnp.where(z > 0, 1, 0) + jnp.where(z < top, 1, 0))

    def remote(src, dst, send, recv, peer):
        return pltpu.make_async_remote_copy(
            src_ref=src, dst_ref=dst, send_sem=send, recv_sem=recv,
            device_id=peer, device_id_type=MESH)

    def piece(kind, part, half, k):
        if kind < 2:
            row = pl.multiple_of(half * (width // 2) + k * wrows, wrows)
            return gu.at[part, kind, pl.ds(row, wrows), :]
        row = pl.multiple_of(part * units + half * (units // 2), units // 2)
        return dn.at[pl.ds(row, units // 2), cols(k)]

    def own_piece(kind, half, k):
        if kind < 2:
            row = pl.multiple_of(half * (width // 2) + k * wrows, wrows)
            return (gate_ref, up_ref)[kind].at[pl.ds(row, wrows), :]
        row = pl.multiple_of(half * (units // 2), units // 2)
        return down_ref.at[pl.ds(row, units // 2), cols(k)]

    def x_copy(kind, k):
        return remote(own_piece(kind, y, k), piece(kind, shard, y, k),
                      x_s.at[kind, k], x_r.at[kind, k], xpeer)

    def y_copy(kind, k):
        got = piece(kind, xshard, y, k)
        return remote(got, got, y_s.at[kind, k], y_r.at[kind, k], ypeer)

    def cx_copy(kind, k):
        got = piece(kind, xshard, y, k)
        return remote(got, got, cx_s.at[kind, k], cx_r.at[kind, k], cpeer)

    def cy_copy(kind, k):
        got = piece(kind, xshard, 1 - y, k)
        return remote(got, got, cy_s.at[kind, k], cy_r.at[kind, k], cpeer)

    own_rows = pl.ds(pl.multiple_of(shard * units, units), units)

    def own_to(kind):
        return (gu.at[shard, 0], gu.at[shard, 1], dn.at[own_rows, :])[kind]

    weights = (gate_ref, up_ref, down_ref)

    def own_core(kind):
        return remote(weights[kind], own_to(kind), co_s.at[kind], co_r.at[kind], cpeer)

    def own_local(kind):
        return pltpu.make_async_copy(weights[kind], own_to(kind), own_sem.at[kind])

    def tok_copy(block, q, up):
        part = tok.at[block, :, cols(q)]
        return remote(part, part, (tu_s if up else td_s).at[block, q], t_r.at[block, q],
                      hi_peer if up else lo_peer)

    def w_copy(block, up):
        part = wts.at[block]
        return remote(part, part, (wu_s if up else wd_s).at[block], w_r.at[block],
                      hi_peer if up else lo_peer)

    def ret_copy(home, q, up, n):
        some = pl.ds(0, n)
        return remote(outbox.at[home, some, cols(q)],
                      (from_lo if up else from_hi).at[home, some, cols(q)],
                      r_s.at[home, q], (lo_r if up else hi_r).at[home, q],
                      hi_peer if up else lo_peer)

    for k in range(AHEAD):
        for kind in (0, 1):
            x_copy(kind, k).start()
    wts[z] = wt_ref[...]

    @pl.when(z < top)
    def _():
        w_copy(z, True).start()

    @pl.when(z > 0)
    def _():
        w_copy(z, False).start()

    had = had_ref[...]

    @pl.loop(0, steps)
    def _(q):
        for b in range(wcols // HB):
            at = pl.ds(pl.multiple_of(q * wcols + b * HB, HB), HB)
            turned = jnp.dot(tok_ref[:, at], had, preferred_element_type=jnp.float32)
            tok[z, :, at] = (turned * (1.0 / HB**0.5)).astype(jnp.bfloat16)

        @pl.when(z < top)
        def _():
            tok_copy(z, q, True).start()

        @pl.when(z > 0)
        def _():
            tok_copy(z, q, False).start()

    for kind in range(3):
        own_local(kind).start()
        own_core(kind).start()

    def relay(r, q):
        lo, hi = z - r, z + r

        @pl.when(lo >= 0)
        def _():
            tok_copy(lo, q, True).wait_recv()

            @pl.when(q == 0)
            def _():
                w_copy(lo, True).wait_recv()

            @pl.when(z < top)
            def _():
                tok_copy(lo, q, True).start()

                @pl.when(q == 0)
                def _():
                    w_copy(lo, True).start()

        @pl.when(hi <= top)
        def _():
            tok_copy(hi, q, False).wait_recv()

            @pl.when(q == 0)
            def _():
                w_copy(hi, False).wait_recv()

            @pl.when(z > 0)
            def _():
                tok_copy(hi, q, False).start()

                @pl.when(q == 0)
                def _():
                    w_copy(hi, False).start()

    def pass_x(kind, k):
        x_copy(kind, k).wait_recv()
        y_copy(kind, k).start()
        cx_copy(kind, k).start()

    def pass_y(kind, k):
        y_copy(kind, k).wait_recv()
        cy_copy(kind, k).start()

    @pl.loop(0, steps)
    def _(k):
        for kind in (0, 1):
            pass_x(kind, k)

            @pl.when(k < steps - AHEAD)
            def _():
                x_copy(kind, k + AHEAD).start()

            @pl.when(k >= steps - AHEAD)
            def _():
                if kind == 0:
                    x_copy(2, 2 * (k - (steps - AHEAD))).start()
                else:
                    x_copy(2, 2 * (k - (steps - AHEAD)) + 1).start()

            @pl.when(k > 0)
            def _():
                pass_y(kind, k - 1)

            t = 2 * k + kind
            relay(t // steps + 1, t % steps)

    for kind in (0, 1):
        pass_y(kind, steps - 1)

    def wait_weights(kind):
        own_local(kind).wait()
        own_core(kind).wait_recv()

        @pl.loop(0, steps)
        def _(k):
            cx_copy(kind, k).wait_recv()
            cy_copy(kind, k).wait_recv()

    low = z < planes // 2

    def home_of(p):
        across = jnp.where(p == 1, jnp.where(low, 2, 1), jnp.where(low, 3, 0))
        beside = jnp.where(low, 1 - z, 5 - z)
        return jnp.where(p == 0, z, jnp.where(p == 3, beside, across))

    end = (z == 0) | (z == top)
    packs = lambda p: end & (p != 0)

    def expert_row(block, expert):
        at = lax.broadcasted_iota(jnp.int32, (8, rows), 0)
        return jnp.sum(jnp.where(at == expert, wts[block], 0.0), axis=0, keepdims=True)

    def slots(weight):
        down, across = (lax.broadcasted_iota(jnp.int32, (rows, rows), d) for d in (0, 1))
        chosen = jnp.where(weight > 0.0, 1.0, 0.0)
        before = jnp.where(down < across, 1.0, 0.0).astype(jnp.bfloat16)
        slot = jnp.dot(jnp.broadcast_to(chosen, (16, rows)).astype(jnp.bfloat16), before,
                       preferred_element_type=jnp.float32)[:1]
        return jnp.where(down.astype(jnp.float32) == slot, chosen, 0.0)

    def make_hidden(p):
        block = home_of(p)
        @pl.loop(0, SHARDS)
        def _(s):
            g = jnp.dot(tok[block], gu[s, 0], preferred_element_type=jnp.float32)
            u = jnp.dot(tok[block], gu[s, 1], preferred_element_type=jnp.float32)
            h = (g / (1.0 + jnp.exp(-g))) * u
            hid[p, :, pl.ds(pl.multiple_of(s * units, units), units)] = h.astype(jnp.bfloat16)

        @pl.when(packs(p))
        def _():
            weight = expert_row(block, z)
            to = slots(weight)
            hid[p] = jnp.dot(to.astype(jnp.bfloat16), hid[p],
                             preferred_element_type=jnp.float32).astype(jnp.bfloat16)
            wcol[p] = jnp.broadcast_to(
                jnp.sum(to * weight, axis=1, keepdims=True), (rows, rows))

        @pl.when(jnp.logical_not(packs(p)))
        def _():
            wcol[p] = jnp.transpose(jnp.broadcast_to(expert_row(block, z), (rows, rows)))

        @pl.when(jnp.logical_not(end))
        def _():
            to = slots(expert_row(block, jnp.where(low, 0, top)))
            place[p] = jnp.transpose(to).astype(jnp.bfloat16)

    def expert_rows(p, q):
        val = jnp.dot(hid[p], dn[:, cols(q)], preferred_element_type=jnp.float32)
        w = wcol[p]
        for b in range(wcols // HB):
            acc[:, b * HB:(b + 1) * HB] = val[:, b * HB:(b + 1) * HB] * w

    def add_in(p, home, q, up):
        source = from_lo if up else from_hi
        packed = (z == 1) if up else (z == top - 1)

        @pl.when(packed)
        def _():
            ret_copy(home, q, up, cap).wait_recv()
            acc[...] += jnp.dot(place[p][:, :cap], source[home, :cap, cols(q)],
                                preferred_element_type=jnp.float32)

        @pl.when(jnp.logical_not(packed))
        def _():
            ret_copy(home, q, up, rows).wait_recv()
            acc[...] += source[home, :, cols(q)].astype(jnp.float32)

    def give_back(p, q):
        home = home_of(p)
        expert_rows(p, q)

        @pl.when((home > z) & (z > 0))
        def _():
            add_in(p, home, q, True)

        @pl.when((home < z) & (z < top))
        def _():
            add_in(p, home, q, False)

        outbox[home, :, cols(q)] = acc[...].astype(jnp.bfloat16)

        @pl.when((home > z) & end)
        def _():
            ret_copy(home, q, True, cap).start()

        @pl.when((home > z) & jnp.logical_not(end))
        def _():
            ret_copy(home, q, True, rows).start()

        @pl.when((home < z) & end)
        def _():
            ret_copy(home, q, False, cap).start()

        @pl.when((home < z) & jnp.logical_not(end))
        def _():
            ret_copy(home, q, False, rows).start()

    wait_weights(0)
    wait_weights(1)
    own_local(2).wait()
    own_core(2).wait_recv()
    make_hidden(1)

    def first_back(q):
        cx_copy(2, q).wait_recv()
        cy_copy(2, q).wait_recv()
        give_back(1, q)

    @pl.loop(0, steps)
    def _(k):
        pass_x(2, k)

        @pl.when(k + 2 * AHEAD < steps)
        def _():
            x_copy(2, k + 2 * AHEAD).start()

        @pl.when(k > 0)
        def _():
            pass_y(2, k - 1)

        relay(planes - 1, k)

        @pl.when(jnp.logical_not(end) & ((k == 1) | (k == 4)))
        def _():
            make_hidden(jnp.where(k == 1, 3, 2))

        @pl.when(k > 1)
        def _():
            first_back(k - 2)

    pass_y(2, steps - 1)
    first_back(steps - 2)
    first_back(steps - 1)

    @pl.when(end)
    def _():
        make_hidden(2)

    lag = jnp.where(end, steps, 2)

    @pl.loop(0, 2 * steps)
    def _(i):
        @pl.when(i < steps)
        def _():
            give_back(2, i)

        @pl.when(end & (i == steps))
        def _():
            make_hidden(3)

        @pl.when((i >= lag) & (i < lag + steps))
        def _():
            give_back(3, i - lag)

    make_hidden(0)

    @pl.loop(0, steps)
    def _(q):
        expert_rows(0, q)

        @pl.when(z > 0)
        def _():
            add_in(0, z, q, True)

        @pl.when(z < top)
        def _():
            add_in(0, z, q, False)

        out_ref[:, cols(q)] = acc[...].astype(jnp.bfloat16)

    for kind in range(3):
        own_core(kind).wait_send()

        @pl.loop(0, steps)
        def _(k):
            x_copy(kind, k).wait_send()
            y_copy(kind, k).wait_send()
            cx_copy(kind, k).wait_send()
            cy_copy(kind, k).wait_send()

    @pl.loop(0, planes)
    def _(block):
        for up in (True, False):
            @pl.when((z < top) & (block <= z) if up else (z > 0) & (block >= z))
            def _():
                w_copy(block, up).wait_send()

                @pl.loop(0, steps)
                def _(q):
                    tok_copy(block, q, up).wait_send()

        for n, mine in ((cap, end), (rows, jnp.logical_not(end))):
            @pl.when((block != z) & mine)
            def _():
                @pl.loop(0, steps)
                def _(q):
                    ret_copy(block, q, True, n).wait_send()


def on_slice(planes, tokens, routes, gates, gate_weight, up_weight, down_weight):
    rows, width = tokens.shape
    units = gate_weight.shape[1]
    steps = 7
    capacity = SHARDS * max(1, 3 * rows * routes.shape[1] // (2 * planes * SHARDS))
    lanes = jnp.arange(8, dtype=jnp.int32)[:, None, None]
    wt = jnp.sum(jnp.where(routes[None] == lanes, gates[None], 0.0), axis=2)
    vmem = pl.BlockSpec(memory_space=pltpu.VMEM)
    anywhere = pl.BlockSpec(memory_space=pl.ANY)
    dma = pltpu.SemaphoreType.DMA
    bf16, f32 = jnp.bfloat16, jnp.float32
    return pl.pallas_call(
        functools.partial(layer_kernel, planes, steps, capacity),
        out_shape=jax.ShapeDtypeStruct((rows, width), bf16),
        in_specs=[vmem] * 3 + [anywhere] * 3,
        out_specs=vmem,
        scratch_shapes=[
            pltpu.VMEM((planes, rows, width), bf16),
            pltpu.VMEM((planes, 8, rows), f32),
            pltpu.VMEM((planes, rows, rows), f32),
            pltpu.VMEM((planes, rows, rows), bf16),
            pltpu.VMEM((SHARDS, 2, width, units), bf16),
            pltpu.VMEM((SHARDS * units, width), bf16),
            pltpu.VMEM((planes, rows, SHARDS * units), bf16),
            pltpu.VMEM((rows, width // steps), f32),
            pltpu.VMEM((planes, rows, width), bf16),
            pltpu.VMEM((planes, rows, width), bf16),
            pltpu.VMEM((planes, rows, width), bf16),
            dma((3,)),
            dma((3, steps)), dma((3, steps)),
            dma((3, steps)), dma((3, steps)),
            dma((3,)), dma((3,)),
            dma((3, steps)), dma((3, steps)),
            dma((3, steps)), dma((3, steps)),
            dma((planes, steps)), dma((planes, steps)), dma((planes, steps)),
            dma((planes,)), dma((planes,)), dma((planes,)),
            dma((planes, steps)), dma((planes, steps)), dma((planes, steps)),
        ],
        compiler_params=pltpu.CompilerParams(
            collective_id=0, has_side_effects=True, vmem_limit_bytes=56 * 2**20
        ),
    )(tokens, wt, hadamard(HB), gate_weight, up_weight, down_weight)


def rotate(tokens):
    row_count, width = tokens.shape
    blocked = tokens.reshape(row_count, width // HB, HB)
    turned = jnp.einsum("tbi,ij->tbj", blocked, hadamard(HB), preferred_element_type=jnp.float32)
    return (turned * (1.0 / HB**0.5)).astype(jnp.bfloat16).reshape(row_count, width)


def on_device(tokens, routes, gates, gate_weight, up_weight, down_weight):
    devices = lax.axis_size("expert")
    resident = devices // SHARDS
    row_count, width = tokens.shape
    per_token = routes.shape[1]
    capacity = SHARDS * max(1, 3 * row_count * per_token // (2 * resident * SHARDS))
    rotated = rotate(tokens)
    flat_routes = routes.reshape(-1)
    onehot = (flat_routes[:, None] == jnp.arange(resident, dtype=jnp.int32)[None, :]).astype(
        jnp.int32
    )
    running = jnp.cumsum(onehot, axis=0) - onehot
    slot = jnp.sum(running * onehot, axis=1)
    target_slot = flat_routes * capacity + slot
    owners = jnp.arange(row_count * per_token, dtype=jnp.int32) // per_token
    owner_table = jnp.full((resident * capacity,), row_count, jnp.int32).at[target_slot].set(owners)
    padded = jnp.concatenate([rotated, jnp.zeros((1, width), jnp.bfloat16)], 0)
    buckets = padded[owner_table].reshape(resident, capacity, width)
    copies = jnp.broadcast_to(buckets[:, None], (resident, SHARDS, capacity, width)).reshape(
        devices, capacity, width
    )
    received = lax.all_to_all(copies, "expert", split_axis=0, concat_axis=0, tiled=True)
    slot_rows = received.reshape(-1, width)
    gate_act = jnp.dot(slot_rows, gate_weight, preferred_element_type=jnp.float32)
    up_act = jnp.dot(slot_rows, up_weight, preferred_element_type=jnp.float32)
    hidden = (jax.nn.silu(gate_act) * up_act).astype(jnp.bfloat16)
    partial_value = jnp.dot(hidden, down_weight, preferred_element_type=jnp.float32).astype(
        jnp.bfloat16
    )
    partial_value = partial_value.reshape(received.shape)
    returned = lax.all_to_all(partial_value, "expert", split_axis=0, concat_axis=0, tiled=True)
    expert_out = jnp.sum(
        returned.reshape(resident, SHARDS, capacity, width).astype(jnp.float32), axis=1
    )
    expert_out = expert_out.reshape(resident * capacity, width)
    picked = expert_out[target_slot].reshape(row_count, per_token, width)
    return jnp.sum(gates[:, :, None] * picked, axis=1).astype(jnp.bfloat16)


def solution(mesh):
    devices = mesh.shape["expert"]
    planes = devices // SHARDS
    body = on_device
    if devices == 16 and mesh.shape["groups"] == 2:
        body = functools.partial(on_slice, planes)
    in_specs = (
        P(("groups", "expert"), None),
        P(("groups", "expert"), None),
        P(("groups", "expert"), None),
        P(None, "expert"),
        P(None, "expert"),
        P("expert", None),
    )
    out_specs = P(("groups", "expert"), None)
    return jax.shard_map(
        body, mesh=mesh, in_specs=in_specs, out_specs=out_specs, check_vma=False
    )
```

```python
import functools
import jax
import jax.numpy as jnp
from jax import lax
from jax.experimental import pallas as pl
from jax.experimental.pallas import tpu as pltpu
from jax.sharding import PartitionSpec as P

HB = 128
SHARDS = 4
AHEAD = 3
MESH = pl.DeviceIdType.MESH


def hadamard(size):
    counter = jnp.arange(size, dtype=jnp.int32)
    parity = jnp.zeros((size, size), jnp.int32)
    for bit_level in range(size.bit_length() - 1):
        parity = parity + (counter[:, None] >> bit_level & counter[None, :] >> bit_level & 1)
    return (1 - 2 * (parity % 2)).astype(jnp.bfloat16)


def layer_kernel(
    planes, steps, cap, tok_ref, wt_ref, had_ref, gate_ref, up_ref, down_ref, out_ref,
    tok, wts, wcol, place, gu, dn, hid, acc, from_lo, from_hi, outbox,
    own_sem, x_s, x_r, y_s, y_r, co_s, co_r, cx_s, cx_r, cy_s, cy_r,
    tu_s, td_s, t_r, wu_s, wd_s, w_r, r_s, lo_r, hi_r,
):
    me = lax.axis_index("expert")
    y = lax.axis_index("groups")
    z, x, c = me // 4, (me // 2) % 2, me % 2
    top = planes - 1
    rows, width = tok_ref.shape
    units = gate_ref.shape[1]
    shard, xshard = 2 * x + c, 2 * (1 - x) + c
    xpeer, cpeer = {"expert": z * 4 + xshard}, {"expert": z * 4 + 2 * x + 1 - c}
    ypeer = {"groups": 1 - y}
    hi_peer, lo_peer = {"expert": me + 4}, {"expert": me - 4}
    wrows, wcols = width // 2 // steps, width // steps
    cols = lambda q: pl.ds(pl.multiple_of(q * wcols, wcols), wcols)

    barrier = pltpu.get_barrier_semaphore()
    for peer in (xpeer, cpeer, ypeer):
        pl.semaphore_signal(barrier, inc=1, device_id=peer, device_id_type=MESH)

    @pl.when(z > 0)
    def _():
        pl.semaphore_signal(barrier, inc=1, device_id=lo_peer, device_id_type=MESH)

    @pl.when(z < top)
    def _():
        pl.semaphore_signal(barrier, inc=1, device_id=hi_peer, device_id_type=MESH)

    pl.semaphore_wait(barrier, 3 + jnp.where(z > 0, 1, 0) + jnp.where(z < top, 1, 0))

    def remote(src, dst, send, recv, peer):
        return pltpu.make_async_remote_copy(
            src_ref=src, dst_ref=dst, send_sem=send, recv_sem=recv,
            device_id=peer, device_id_type=MESH)

    def piece(kind, part, half, k):
        if kind < 2:
            row = pl.multiple_of(half * (width // 2) + k * wrows, wrows)
            return gu.at[part, kind, pl.ds(row, wrows), :]
        row = pl.multiple_of(part * units + half * (units // 2), units // 2)
        return dn.at[pl.ds(row, units // 2), cols(k)]

    def own_piece(kind, half, k):
        if kind < 2:
            row = pl.multiple_of(half * (width // 2) + k * wrows, wrows)
            return (gate_ref, up_ref)[kind].at[pl.ds(row, wrows), :]
        row = pl.multiple_of(half * (units // 2), units // 2)
        return down_ref.at[pl.ds(row, units // 2), cols(k)]

    def x_copy(kind, k):
        return remote(own_piece(kind, y, k), piece(kind, shard, y, k),
                      x_s.at[kind, k], x_r.at[kind, k], xpeer)

    def y_copy(kind, k):
        got = piece(kind, xshard, y, k)
        return remote(got, got, y_s.at[kind, k], y_r.at[kind, k], ypeer)

    def cx_copy(kind, k):
        got = piece(kind, xshard, y, k)
        return remote(got, got, cx_s.at[kind, k], cx_r.at[kind, k], cpeer)

    def cy_copy(kind, k):
        got = piece(kind, xshard, 1 - y, k)
        return remote(got, got, cy_s.at[kind, k], cy_r.at[kind, k], cpeer)

    own_rows = pl.ds(pl.multiple_of(shard * units, units), units)

    def own_to(kind):
        return (gu.at[shard, 0], gu.at[shard, 1], dn.at[own_rows, :])[kind]

    weights = (gate_ref, up_ref, down_ref)

    def own_core(kind):
        return remote(weights[kind], own_to(kind), co_s.at[kind], co_r.at[kind], cpeer)

    def own_local(kind):
        return pltpu.make_async_copy(weights[kind], own_to(kind), own_sem.at[kind])

    def tok_copy(block, q, up):
        part = tok.at[block, :, cols(q)]
        return remote(part, part, (tu_s if up else td_s).at[block, q], t_r.at[block, q],
                      hi_peer if up else lo_peer)

    def w_copy(block, up):
        part = wts.at[block]
        return remote(part, part, (wu_s if up else wd_s).at[block], w_r.at[block],
                      hi_peer if up else lo_peer)

    def ret_copy(home, q, up, n):
        some = pl.ds(0, n)
        return remote(outbox.at[home, some, cols(q)],
                      (from_lo if up else from_hi).at[home, some, cols(q)],
                      r_s.at[home, q], (lo_r if up else hi_r).at[home, q],
                      hi_peer if up else lo_peer)

    for k in range(AHEAD):
        for kind in (0, 1):
            x_copy(kind, k).start()
    wts[z] = wt_ref[...]

    @pl.when(z < top)
    def _():
        w_copy(z, True).start()

    @pl.when(z > 0)
    def _():
        w_copy(z, False).start()

    had = had_ref[...]

    @pl.loop(0, steps)
    def _(q):
        for b in range(wcols // HB):
            at = pl.ds(pl.multiple_of(q * wcols + b * HB, HB), HB)
            turned = jnp.dot(tok_ref[:, at], had, preferred_element_type=jnp.float32)
            tok[z, :, at] = (turned * (1.0 / HB**0.5)).astype(jnp.bfloat16)

        @pl.when(z < top)
        def _():
            tok_copy(z, q, True).start()

        @pl.when(z > 0)
        def _():
            tok_copy(z, q, False).start()

    for kind in range(3):
        own_local(kind).start()
        own_core(kind).start()

    def relay(r, q):
        lo, hi = z - r, z + r

        @pl.when(lo >= 0)
        def _():
            tok_copy(lo, q, True).wait_recv()

            @pl.when(q == 0)
            def _():
                w_copy(lo, True).wait_recv()

            @pl.when(z < top)
            def _():
                tok_copy(lo, q, True).start()

                @pl.when(q == 0)
                def _():
                    w_copy(lo, True).start()

        @pl.when(hi <= top)
        def _():
            tok_copy(hi, q, False).wait_recv()

            @pl.when(q == 0)
            def _():
                w_copy(hi, False).wait_recv()

            @pl.when(z > 0)
            def _():
                tok_copy(hi, q, False).start()

                @pl.when(q == 0)
                def _():
                    w_copy(hi, False).start()

    def pass_x(kind, k):
        x_copy(kind, k).wait_recv()
        y_copy(kind, k).start()
        cx_copy(kind, k).start()

    def pass_y(kind, k):
        y_copy(kind, k).wait_recv()
        cy_copy(kind, k).start()

    @pl.loop(0, steps)
    def _(k):
        for kind in (0, 1):
            pass_x(kind, k)

            @pl.when(k < steps - AHEAD)
            def _():
                x_copy(kind, k + AHEAD).start()

            @pl.when(k >= steps - AHEAD)
            def _():
                if kind == 0:
                    x_copy(2, 2 * (k - (steps - AHEAD))).start()
                else:
                    x_copy(2, 2 * (k - (steps - AHEAD)) + 1).start()

            @pl.when(k > 0)
            def _():
                pass_y(kind, k - 1)

            t = 2 * k + kind
            relay(t // steps + 1, t % steps)

    for kind in (0, 1):
        pass_y(kind, steps - 1)

    def wait_weights(kind):
        own_local(kind).wait()
        own_core(kind).wait_recv()

        @pl.loop(0, steps)
        def _(k):
            cx_copy(kind, k).wait_recv()
            cy_copy(kind, k).wait_recv()

    low = z < planes // 2

    def home_of(p):
        across = jnp.where(p == 1, jnp.where(low, 2, 1), jnp.where(low, 3, 0))
        beside = jnp.where(low, 1 - z, 5 - z)
        return jnp.where(p == 0, z, jnp.where(p == 3, beside, across))

    end = (z == 0) | (z == top)
    packs = lambda p: end & (p != 0)

    def expert_row(block, expert):
        at = lax.broadcasted_iota(jnp.int32, (8, rows), 0)
        return jnp.sum(jnp.where(at == expert, wts[block], 0.0), axis=0, keepdims=True)

    def slots(weight):
        down, across = (lax.broadcasted_iota(jnp.int32, (rows, rows), d) for d in (0, 1))
        chosen = jnp.where(weight > 0.0, 1.0, 0.0)
        before = jnp.where(down < across, 1.0, 0.0).astype(jnp.bfloat16)
        slot = jnp.dot(jnp.broadcast_to(chosen, (16, rows)).astype(jnp.bfloat16), before,
                       preferred_element_type=jnp.float32)[:1]
        return jnp.where(down.astype(jnp.float32) == slot, chosen, 0.0)

    def make_hidden(p):
        block = home_of(p)
        @pl.loop(0, SHARDS)
        def _(s):
            g = jnp.dot(tok[block], gu[s, 0], preferred_element_type=jnp.float32)
            u = jnp.dot(tok[block], gu[s, 1], preferred_element_type=jnp.float32)
            h = (g / (1.0 + jnp.exp(-g))) * u
            hid[p, :, pl.ds(pl.multiple_of(s * units, units), units)] = h.astype(jnp.bfloat16)

        @pl.when(packs(p))
        def _():
            weight = expert_row(block, z)
            to = slots(weight)
            hid[p] = jnp.dot(to.astype(jnp.bfloat16), hid[p],
                             preferred_element_type=jnp.float32).astype(jnp.bfloat16)
            wcol[p] = jnp.broadcast_to(
                jnp.sum(to * weight, axis=1, keepdims=True), (rows, rows))

        @pl.when(jnp.logical_not(packs(p)))
        def _():
            wcol[p] = jnp.transpose(jnp.broadcast_to(expert_row(block, z), (rows, rows)))

        @pl.when(jnp.logical_not(end))
        def _():
            to = slots(expert_row(block, jnp.where(low, 0, top)))
            place[p] = jnp.transpose(to).astype(jnp.bfloat16)

    def expert_rows(p, q):
        val = jnp.dot(hid[p], dn[:, cols(q)], preferred_element_type=jnp.float32)
        w = wcol[p]
        for b in range(wcols // HB):
            acc[:, b * HB:(b + 1) * HB] = val[:, b * HB:(b + 1) * HB] * w

    def add_in(p, home, q, up):
        source = from_lo if up else from_hi
        packed = (z == 1) if up else (z == top - 1)

        @pl.when(packed)
        def _():
            ret_copy(home, q, up, cap).wait_recv()
            acc[...] += jnp.dot(place[p][:, :cap], source[home, :cap, cols(q)],
                                preferred_element_type=jnp.float32)

        @pl.when(jnp.logical_not(packed))
        def _():
            ret_copy(home, q, up, rows).wait_recv()
            acc[...] += source[home, :, cols(q)].astype(jnp.float32)

    def give_back(p, q):
        home = home_of(p)
        expert_rows(p, q)

        @pl.when((home > z) & (z > 0))
        def _():
            add_in(p, home, q, True)

        @pl.when((home < z) & (z < top))
        def _():
            add_in(p, home, q, False)

        outbox[home, :, cols(q)] = acc[...].astype(jnp.bfloat16)

        @pl.when((home > z) & end)
        def _():
            ret_copy(home, q, True, cap).start()

        @pl.when((home > z) & jnp.logical_not(end))
        def _():
            ret_copy(home, q, True, rows).start()

        @pl.when((home < z) & end)
        def _():
            ret_copy(home, q, False, cap).start()

        @pl.when((home < z) & jnp.logical_not(end))
        def _():
            ret_copy(home, q, False, rows).start()

    wait_weights(0)
    wait_weights(1)
    own_local(2).wait()
    own_core(2).wait_recv()
    make_hidden(1)

    def first_back(q):
        cx_copy(2, q).wait_recv()
        cy_copy(2, q).wait_recv()
        give_back(1, q)

    @pl.loop(0, steps)
    def _(k):
        pass_x(2, k)

        @pl.when(k + 2 * AHEAD < steps)
        def _():
            x_copy(2, k + 2 * AHEAD).start()

        @pl.when(k > 0)
        def _():
            pass_y(2, k - 1)

        relay(planes - 1, k)

        @pl.when((k == 1) | (jnp.logical_not(end) & (k == 4)))
        def _():
            make_hidden(jnp.where(k == 1, 3, 2))

        @pl.when(k > 1)
        def _():
            first_back(k - 2)

    pass_y(2, steps - 1)
    first_back(steps - 2)
    first_back(steps - 1)

    @pl.when(end)
    def _():
        give_back(3, 0)
        give_back(3, 1)
        make_hidden(2)

    lag = jnp.where(end, steps, 2)

    @pl.loop(0, 2 * steps)
    def _(i):
        @pl.when(i < steps)
        def _():
            give_back(2, i)

        @pl.when((i >= lag + jnp.where(end, 2, 0)) & (i < lag + steps))
        def _():
            give_back(3, i - lag)

    make_hidden(0)

    @pl.loop(0, steps)
    def _(q):
        expert_rows(0, q)

        @pl.when(z > 0)
        def _():
            add_in(0, z, q, True)

        @pl.when(z < top)
        def _():
            add_in(0, z, q, False)

        out_ref[:, cols(q)] = acc[...].astype(jnp.bfloat16)

    for kind in range(3):
        own_core(kind).wait_send()

        @pl.loop(0, steps)
        def _(k):
            x_copy(kind, k).wait_send()
            y_copy(kind, k).wait_send()
            cx_copy(kind, k).wait_send()
            cy_copy(kind, k).wait_send()

    @pl.loop(0, planes)
    def _(block):
        for up in (True, False):
            @pl.when((z < top) & (block <= z) if up else (z > 0) & (block >= z))
            def _():
                w_copy(block, up).wait_send()

                @pl.loop(0, steps)
                def _(q):
                    tok_copy(block, q, up).wait_send()

        for n, mine in ((cap, end), (rows, jnp.logical_not(end))):
            @pl.when((block != z) & mine)
            def _():
                @pl.loop(0, steps)
                def _(q):
                    ret_copy(block, q, True, n).wait_send()


def on_slice(planes, tokens, routes, gates, gate_weight, up_weight, down_weight):
    rows, width = tokens.shape
    units = gate_weight.shape[1]
    steps = 7
    capacity = SHARDS * max(1, 3 * rows * routes.shape[1] // (2 * planes * SHARDS))
    lanes = jnp.arange(8, dtype=jnp.int32)[:, None, None]
    wt = jnp.sum(jnp.where(routes[None] == lanes, gates[None], 0.0), axis=2)
    vmem = pl.BlockSpec(memory_space=pltpu.VMEM)
    anywhere = pl.BlockSpec(memory_space=pl.ANY)
    dma = pltpu.SemaphoreType.DMA
    bf16, f32 = jnp.bfloat16, jnp.float32
    return pl.pallas_call(
        functools.partial(layer_kernel, planes, steps, capacity),
        out_shape=jax.ShapeDtypeStruct((rows, width), bf16),
        in_specs=[vmem] * 3 + [anywhere] * 3,
        out_specs=vmem,
        scratch_shapes=[
            pltpu.VMEM((planes, rows, width), bf16),
            pltpu.VMEM((planes, 8, rows), f32),
            pltpu.VMEM((planes, rows, rows), f32),
            pltpu.VMEM((planes, rows, rows), bf16),
            pltpu.VMEM((SHARDS, 2, width, units), bf16),
            pltpu.VMEM((SHARDS * units, width), bf16),
            pltpu.VMEM((planes, rows, SHARDS * units), bf16),
            pltpu.VMEM((rows, width // steps), f32),
            pltpu.VMEM((planes, rows, width), bf16),
            pltpu.VMEM((planes, rows, width), bf16),
            pltpu.VMEM((planes, rows, width), bf16),
            dma((3,)),
            dma((3, steps)), dma((3, steps)),
            dma((3, steps)), dma((3, steps)),
            dma((3,)), dma((3,)),
            dma((3, steps)), dma((3, steps)),
            dma((3, steps)), dma((3, steps)),
            dma((planes, steps)), dma((planes, steps)), dma((planes, steps)),
            dma((planes,)), dma((planes,)), dma((planes,)),
            dma((planes, steps)), dma((planes, steps)), dma((planes, steps)),
        ],
        compiler_params=pltpu.CompilerParams(
            collective_id=0, has_side_effects=True, vmem_limit_bytes=56 * 2**20
        ),
    )(tokens, wt, hadamard(HB), gate_weight, up_weight, down_weight)


def rotate(tokens):
    row_count, width = tokens.shape
    blocked = tokens.reshape(row_count, width // HB, HB)
    turned = jnp.einsum("tbi,ij->tbj", blocked, hadamard(HB), preferred_element_type=jnp.float32)
    return (turned * (1.0 / HB**0.5)).astype(jnp.bfloat16).reshape(row_count, width)


def on_device(tokens, routes, gates, gate_weight, up_weight, down_weight):
    devices = lax.axis_size("expert")
    resident = devices // SHARDS
    row_count, width = tokens.shape
    per_token = routes.shape[1]
    capacity = SHARDS * max(1, 3 * row_count * per_token // (2 * resident * SHARDS))
    rotated = rotate(tokens)
    flat_routes = routes.reshape(-1)
    onehot = (flat_routes[:, None] == jnp.arange(resident, dtype=jnp.int32)[None, :]).astype(
        jnp.int32
    )
    running = jnp.cumsum(onehot, axis=0) - onehot
    slot = jnp.sum(running * onehot, axis=1)
    target_slot = flat_routes * capacity + slot
    owners = jnp.arange(row_count * per_token, dtype=jnp.int32) // per_token
    owner_table = jnp.full((resident * capacity,), row_count, jnp.int32).at[target_slot].set(owners)
    padded = jnp.concatenate([rotated, jnp.zeros((1, width), jnp.bfloat16)], 0)
    buckets = padded[owner_table].reshape(resident, capacity, width)
    copies = jnp.broadcast_to(buckets[:, None], (resident, SHARDS, capacity, width)).reshape(
        devices, capacity, width
    )
    received = lax.all_to_all(copies, "expert", split_axis=0, concat_axis=0, tiled=True)
    slot_rows = received.reshape(-1, width)
    gate_act = jnp.dot(slot_rows, gate_weight, preferred_element_type=jnp.float32)
    up_act = jnp.dot(slot_rows, up_weight, preferred_element_type=jnp.float32)
    hidden = (jax.nn.silu(gate_act) * up_act).astype(jnp.bfloat16)
    partial_value = jnp.dot(hidden, down_weight, preferred_element_type=jnp.float32).astype(
        jnp.bfloat16
    )
    partial_value = partial_value.reshape(received.shape)
    returned = lax.all_to_all(partial_value, "expert", split_axis=0, concat_axis=0, tiled=True)
    expert_out = jnp.sum(
        returned.reshape(resident, SHARDS, capacity, width).astype(jnp.float32), axis=1
    )
    expert_out = expert_out.reshape(resident * capacity, width)
    picked = expert_out[target_slot].reshape(row_count, per_token, width)
    return jnp.sum(gates[:, :, None] * picked, axis=1).astype(jnp.bfloat16)


def solution(mesh):
    devices = mesh.shape["expert"]
    planes = devices // SHARDS
    body = on_device
    if devices == 16 and mesh.shape["groups"] == 2:
        body = functools.partial(on_slice, planes)
    in_specs = (
        P(("groups", "expert"), None),
        P(("groups", "expert"), None),
        P(("groups", "expert"), None),
        P(None, "expert"),
        P(None, "expert"),
        P("expert", None),
    )
    out_specs = P(("groups", "expert"), None)
    return jax.shard_map(
        body, mesh=mesh, in_specs=in_specs, out_specs=out_specs, check_vma=False
    )
```
